32 devices in a mesh: groups: 2 (over y), dp: 16 (over z, x, core).
Axes of the slice: x: 2, y: 2, z: 4, core: 2. Of those that a mesh axis runs over, the one named last changes fastest.
Arguments:
- stored_inputs: bfloat16 [64, 128, 14336], P(('groups', 'dp')), parts along dimension 0, may hold values from -6 to 6
- output_grads: bfloat16 [64, 128, 4096], P(('groups', 'dp')), parts along dimension 0, may hold values from -6 to 6
- basis_in: bfloat16 [14336, 64], replicated, may hold values from -0.046875 to 0.046875
- basis_out: bfloat16 [4096, 64], replicated, may hold values from -0.09375 to 0.09375
- ex_weight: float32 [64], P(('groups', 'dp')), parts along dimension 0, may hold values from 0.5 to 18, as said below
Outputs:
- fisher: float32 [8192, 1024], P(('groups', 'dp')), parts along dimension 0
- proj_grads: bfloat16 [64, 4096], P(('groups', 'dp')), parts along dimension 0
The draws below stay inside these ranges and needn't reach their ends.
There are 2 independent parts, one for each index of `groups`. The reference program is written for one: setup_inputs(seed, part) draws one part's arguments, and reference() takes and returns one part's arrays. A program takes and returns all parts, laid end to end along the dimension named above; an argument that names none is the same for every part. Nothing has to cross between parts.
Inputs may be any that keep to these rules, and one draw needn't show every extreme that they name: `ex_weight`: each example's importance weight is positive.
All inputs are finite; a program needn't handle non-finite values.
Results may differ from the reference program's by a relative error of at most 0.0065.
Values sent between devices are 32-bit elements; how exact they have to be, the bound alone decides.
A program may use at most 128 MiB of HBM per device.

```python
import jax
import jax.numpy as jnp
from jax import lax

D = 4096
FF = 14336
R_IN = 64
R_OUT = 64
SEQ = 128
FCOLS = 1024
EXAMPLES = 32


def draw_ex_weight(key, part):
    key = jax.random.fold_in(key, 7)
    position = jnp.arange(EXAMPLES, dtype=jnp.float32) / max(EXAMPLES - 1, 1)
    rising = 1.0 + 2.0 * position
    factor = jnp.exp(jax.random.uniform(key, (EXAMPLES,), jnp.float32, -0.69, 0.69))
    return rising * factor


def steps_of(stream_key, shape, cuts, smallest, largest):
    factor_of = 1.0
    for dim, parts in cuts:
        heights = jax.random.uniform(jax.random.fold_in(jax.random.fold_in(stream_key, 6), dim), (parts,), jnp.float32, smallest / len(cuts), largest / len(cuts))
        factor_of = factor_of * jnp.repeat(jnp.exp(heights), shape[dim] // parts).reshape((-1,) + (1,) * (len(shape) - 1 - dim))
    return factor_of


def gaussian(rng, extent, deviation, limit, split=(), kind=jnp.bfloat16):
    level = steps_of(rng, extent, split, -0.22, 0.18) if split else 1.0
    values = jax.random.normal(rng, extent, jnp.float32) * deviation * level
    return jnp.minimum(jnp.maximum(values, -limit), limit).astype(kind)


def setup_inputs(seed: int = 0, part: int = 0) -> dict:
    streams_of = jax.random.split(jax.random.key(seed), 6)
    own_keys = jax.random.split(jax.random.fold_in(streams_of[5], part), 6)
    stored_inputs = gaussian(own_keys[0], (EXAMPLES, SEQ, FF), 1.0, 6.0, ((0, 16),))
    output_grads = gaussian(own_keys[1], (EXAMPLES, SEQ, D), 1.0, 6.0, ((0, 16),))
    basis_in = gaussian(streams_of[2], (FF, R_IN), FF ** -0.5, 0.046875)
    basis_out = gaussian(streams_of[3], (D, R_OUT), D ** -0.5, 0.09375)
    ex_weight = draw_ex_weight(jax.random.fold_in(jax.random.fold_in(streams_of[5], part), 71), part)
    return {"stored_inputs": stored_inputs, "output_grads": output_grads, "basis_in": basis_in, "basis_out": basis_out, "ex_weight": ex_weight}


epsilon = 1e-6


def reference(stored_inputs, output_grads, basis_in, basis_out, ex_weight):
    proj_in = jnp.dot(stored_inputs.reshape(EXAMPLES * SEQ, FF), basis_in, preferred_element_type=jnp.float32).astype(jnp.bfloat16)
    proj_out = jnp.dot(output_grads.reshape(EXAMPLES * SEQ, D), basis_out, preferred_element_type=jnp.float32).astype(jnp.bfloat16)
    proj_in = proj_in.reshape(EXAMPLES, SEQ, R_IN).astype(jnp.float32)
    proj_out = proj_out.reshape(EXAMPLES, SEQ, R_OUT).astype(jnp.float32)
    blocks = jnp.einsum("eto,eti->eoi", proj_out, proj_in, precision=lax.Precision.HIGHEST)
    flat = blocks.reshape(EXAMPLES, R_OUT * R_IN)
    weighted = flat * ex_weight[:, None]
    raw = jnp.dot(weighted.T, flat[:, :FCOLS], precision=lax.Precision.HIGHEST, preferred_element_type=jnp.float32)
    trace_total = jnp.sum(weighted * flat)
    fisher = raw * (R_OUT * R_IN / (trace_total + epsilon))
    return fisher, flat.astype(jnp.bfloat16)
```

```python
import functools

import jax
import jax.numpy as jnp
from jax import lax
from jax.experimental import pallas as pl
from jax.experimental.pallas import tpu as pltpu
from jax.sharding import PartitionSpec as P

FCOLS = 1024
LANES = 128
EPSILON = 1e-6
NT = (((1,), (1,)), ((), ()))
TN = (((0,), (0,)), ((), ()))


def cut(total, most):
    tiles = total // LANES
    count = -(-total // most)
    edges = [tiles * i // count * LANES for i in range(count + 1)]
    return list(zip(edges[:-1], edges[1:]))


def split(value):
    high = value.astype(jnp.bfloat16)
    return high, (value - high.astype(jnp.float32)).astype(jnp.bfloat16)


def kernel(n, ex, own_rows, x_cuts, g_cuts, x_ref, g_ref, bi_ref, bo_ref, w_ref, fisher_ref, pg_ref,
           xv, gv, biv, bov, wv, blk, flatv, msg, recv, outv, pgv,
           xs, bis, gs, bos, send_sem, recv_sem, out_sem, pg_sem, w_sem):
    me = lax.axis_index("dp")
    tokens = x_ref.shape[0] // ex
    rank_in, rank_out = bi_ref.shape[0], bo_ref.shape[0]
    left = FCOLS // LANES
    flat_rows = rank_in * rank_out // LANES
    seg = max(1, own_rows // LANES)
    stat = ex * (left + seg)

    def load(ref, buf, sem, i, lo, hi):
        return pltpu.make_async_copy(ref.at[:, lo:hi], buf.at[:, lo:hi], sem.at[i])

    for i, (lo, hi) in enumerate(g_cuts):
        load(bo_ref, bov, bos, i, lo, hi).start()
        load(g_ref, gv, gs, i, lo, hi).start()
    for i, (lo, hi) in enumerate(x_cuts):
        load(bi_ref, biv, bis, i, lo, hi).start()
        load(x_ref, xv, xs, i, lo, hi).start()

    w_copy = pltpu.make_async_copy(w_ref, wv, w_sem)
    w_copy.start()

    barrier = pltpu.get_barrier_semaphore()
    for k in range(1, n):
        pl.semaphore_signal(barrier, inc=1, device_id={"dp": lax.rem(me + k, n)}, device_id_type=pl.DeviceIdType.MESH)

    def project(ref, buf, sem, b_ref, b_buf, b_sem, cuts):
        total = None
        for i, (lo, hi) in enumerate(cuts):
            load(b_ref, b_buf, b_sem, i, lo, hi).wait()
            load(ref, buf, sem, i, lo, hi).wait()
            term = lax.dot_general(buf[:, lo:hi], b_buf[:, lo:hi], NT, preferred_element_type=jnp.float32)
            total = term if total is None else total + term
        return total.astype(jnp.bfloat16)

    proj_out = project(g_ref, gv, gs, bo_ref, bov, bos, g_cuts)
    proj_in = project(x_ref, xv, xs, bi_ref, biv, bis, x_cuts)

    w_copy.wait()
    trace = None
    for e in range(ex):
        span = slice(e * tokens, (e + 1) * tokens)
        blk[e] = lax.dot_general(proj_out[span], proj_in[span], TN, preferred_element_type=jnp.float32)
    for e in range(ex):
        per = LANES // rank_in
        flat = jnp.concatenate([blk[e, pl.ds(p, flat_rows, per), :] for p in range(per)], axis=1)
        weighted = flat * wv[e]
        flatv[e] = flat
        term = jnp.sum(weighted * flat, axis=0, keepdims=True)
        trace = term if trace is None else trace + term
        for d in range(n):
            first = d * own_rows // LANES
            msg[d, e * left:(e + 1) * left] = flat[:left]
            msg[d, ex * left + e * seg:ex * left + (e + 1) * seg] = weighted[first:first + seg]
    for d in range(n):
        msg[d, stat:stat + 1] = trace

    pl.semaphore_wait(barrier, n - 1)

    def send(k):
        to = lax.rem(me + k, n)
        return pltpu.make_async_remote_copy(
            src_ref=msg.at[to], dst_ref=recv.at[me], send_sem=send_sem.at[k], recv_sem=recv_sem.at[me],
            device_id={"dp": to}, device_id_type=pl.DeviceIdType.MESH)

    def arrival(k):
        source = lax.rem(me + n - k, n)
        return pltpu.make_async_remote_copy(
            src_ref=msg.at[me], dst_ref=recv.at[source], send_sem=send_sem.at[k], recv_sem=recv_sem.at[source],
            device_id={"dp": source}, device_id_type=pl.DeviceIdType.MESH)

    for k in range(1, n):
        send(k).start()
    recv[me] = msg[me]
    for q in range(flat_rows):
        pgv[:, q * LANES:(q + 1) * LANES] = flatv[:, q, :].astype(jnp.bfloat16)
    pg_copy = pltpu.make_async_copy(pgv, pg_ref, pg_sem)
    pg_copy.start()
    for k in range(1, n):
        arrival(k).wait_recv()

    def rows(first, step):
        return jnp.concatenate([recv[:, first + e * step, :] for e in range(ex)], axis=0)

    total = jnp.sum(recv[:, stat, :], keepdims=True)
    scale = (rank_in * rank_out) / (total + EPSILON)
    lhs = jnp.concatenate([rows(ex * left + q, seg) for q in range(seg)], axis=1) * scale
    lhs_high, lhs_low = split(lhs)
    lhs = jnp.concatenate([lhs_high, lhs_high, lhs_low], axis=0)
    rhs_high, rhs_low = split(jnp.concatenate([rows(j, left) for j in range(left)], axis=1))
    rhs = jnp.concatenate([rhs_high, rhs_low, rhs_high], axis=0)
    copies = []
    if own_rows % LANES:
        outv[...] = lax.dot_general(lhs, rhs, TN, preferred_element_type=jnp.float32)
        first = pl.multiple_of(lax.rem(me * own_rows, LANES), own_rows)
        copies.append(pltpu.make_async_copy(outv.at[pl.ds(first, own_rows)], fisher_ref, out_sem.at[0]))
        copies[-1].start()
    else:
        for i in range(seg):
            span = slice(i * LANES, (i + 1) * LANES)
            outv[span] = lax.dot_general(lhs[:, span], rhs, TN, preferred_element_type=jnp.float32)
            copies.append(pltpu.make_async_copy(outv.at[span], fisher_ref.at[span], out_sem.at[i]))
            copies[-1].start()
    for k in range(1, n):
        send(k).wait_send()
    pg_copy.wait()
    for copy in copies:
        copy.wait()


def local(n, stored_inputs, output_grads, basis_in, basis_out, ex_weight):
    ex, seq, ff = stored_inputs.shape
    width = output_grads.shape[2]
    rank_in, rank_out = basis_in.shape[1], basis_out.shape[1]
    flat_width = rank_in * rank_out
    own_rows = flat_width // n
    seg = max(1, own_rows // LANES)
    x_cuts, g_cuts = cut(ff, 2048), cut(width, 2048)
    msg_rows = -(-(ex * (FCOLS // LANES + seg) + 1) // 8) * 8
    any_spec = pl.BlockSpec(memory_space=pl.ANY)
    bf16, f32 = jnp.bfloat16, jnp.float32
    dma = pltpu.SemaphoreType.DMA
    return pl.pallas_call(
        functools.partial(kernel, n, ex, own_rows, x_cuts, g_cuts),
        out_shape=(jax.ShapeDtypeStruct((own_rows, FCOLS), f32), jax.ShapeDtypeStruct((ex, flat_width), bf16)),
        in_specs=[pl.BlockSpec(memory_space=pltpu.HBM)] * 5,
        out_specs=(any_spec, any_spec),
        scratch_shapes=[
            pltpu.VMEM((ex * seq, ff), bf16),
            pltpu.VMEM((ex * seq, width), bf16),
            pltpu.VMEM((rank_in, ff), bf16),
            pltpu.VMEM((rank_out, width), bf16),
            pltpu.SMEM((ex,), f32),
            pltpu.VMEM((ex, rank_out, rank_in), f32),
            pltpu.VMEM((ex, flat_width // LANES, LANES), f32),
            pltpu.VMEM((n, msg_rows, LANES), f32),
            pltpu.VMEM((n, msg_rows, LANES), f32),
            pltpu.VMEM((seg * LANES, FCOLS), f32),
            pltpu.VMEM((ex, flat_width), bf16),
            dma((len(x_cuts),)), dma((len(x_cuts),)), dma((len(g_cuts),)), dma((len(g_cuts),)),
            dma((n,)), dma((n,)), dma((seg,)), dma(()), dma(()),
        ],
        compiler_params=pltpu.CompilerParams(
            collective_id=0, has_side_effects=True, vmem_limit_bytes=48 * 1024 * 1024),
    )(stored_inputs.reshape(ex * seq, ff), output_grads.reshape(ex * seq, width), basis_in.T, basis_out.T, ex_weight)


def solution(mesh):
    in_specs = (
        P(("groups", "dp"), None, None),
        P(("groups", "dp"), None, None),
        P(),
        P(),
        P(("groups", "dp")),
    )
    out_specs = (P(("groups", "dp"), None), P(("groups", "dp"), None))
    return jax.shard_map(functools.partial(local, mesh.shape["dp"]), mesh=mesh, in_specs=in_specs, out_specs=out_specs, check_vma=False)
```

```python
import functools

import jax
import jax.numpy as jnp
from jax import lax
from jax.experimental import pallas as pl
from jax.experimental.pallas import tpu as pltpu
from jax.sharding import PartitionSpec as P

FCOLS = 1024
LANES = 128
WINDOW = 4
EPSILON = 1e-6
NT = (((1,), (1,)), ((), ()))
TN = (((0,), (0,)), ((), ()))


def cut(total, most):
    tiles = total // LANES
    count = -(-total // most)
    edges = [tiles * i // count * LANES for i in range(count + 1)]
    return list(zip(edges[:-1], edges[1:]))


def split(value):
    high = value.astype(jnp.bfloat16)
    return high, (value - high.astype(jnp.float32)).astype(jnp.bfloat16)


def exchange(n, ex, own_rows, x_cuts, g_cuts, x_ref, g_ref, bi_ref, bo_ref, w_ref, recv, pg_ref,
           xv, gv, biv, bov, wv, blk, flatv, msg, pgv,
           xs, bis, gs, bos, send_sem, recv_sem, own_sem, pg_sem, w_sem):
    me = lax.axis_index("dp")
    tokens = x_ref.shape[0] // ex
    rank_in, rank_out = bi_ref.shape[0], bo_ref.shape[0]
    left = FCOLS // LANES
    flat_rows = rank_in * rank_out // LANES
    seg = max(1, own_rows // LANES)
    stat = ex * (left + seg)

    def load(ref, buf, sem, i, lo, hi):
        return pltpu.make_async_copy(ref.at[:, lo:hi], buf.at[:, lo:hi], sem.at[i])

    chunks = [((x_ref, xv, xs), (bi_ref, biv, bis), i, lo, hi) for i, (lo, hi) in enumerate(x_cuts)]
    chunks += [((g_ref, gv, gs), (bo_ref, bov, bos), i, lo, hi) for i, (lo, hi) in enumerate(g_cuts)]

    def issue(at):
        if at < len(chunks):
            data, basis, i, lo, hi = chunks[at]
            load(*basis, i, lo, hi).start()
            load(*data, i, lo, hi).start()

    for at in range(WINDOW):
        issue(at)
    w_copy = pltpu.make_async_copy(w_ref, wv, w_sem)
    w_copy.start()

    barrier = pltpu.get_barrier_semaphore()
    for k in range(1, n):
        pl.semaphore_signal(barrier, inc=1, device_id={"dp": lax.rem(me + k, n)}, device_id_type=pl.DeviceIdType.MESH)

    totals = {}
    for at, (data, basis, i, lo, hi) in enumerate(chunks):
        load(*basis, i, lo, hi).wait()
        load(*data, i, lo, hi).wait()
        issue(at + WINDOW)
        term = lax.dot_general(data[1][:, lo:hi], basis[1][:, lo:hi], NT, preferred_element_type=jnp.float32)
        side = "in" if at < len(x_cuts) else "out"
        totals[side] = totals[side] + term if side in totals else term
    proj_in, proj_out = (totals[side].astype(jnp.bfloat16) for side in ("in", "out"))

    w_copy.wait()
    trace = None
    for e in range(ex):
        span = slice(e * tokens, (e + 1) * tokens)
        blk[e] = lax.dot_general(proj_out[span], proj_in[span], TN, preferred_element_type=jnp.float32)
    for e in range(ex):
        per = LANES // rank_in
        flat = jnp.concatenate([blk[e, pl.ds(p, flat_rows, per), :] for p in range(per)], axis=1)
        weighted = flat * wv[e]
        flatv[e] = flat
        term = jnp.sum(weighted * flat, axis=0, keepdims=True)
        trace = term if trace is None else trace + term
        for d in range(n):
            first = d * own_rows // LANES
            msg[d, e * left:(e + 1) * left] = flat[:left]
            msg[d, ex * left + e * seg:ex * left + (e + 1) * seg] = weighted[first:first + seg]
    for d in range(n):
        msg[d, stat:stat + 1] = trace

    pl.semaphore_wait(barrier, n - 1)

    def send(k):
        to = lax.rem(me + k, n)
        return pltpu.make_async_remote_copy(
            src_ref=msg.at[to], dst_ref=recv.at[me], send_sem=send_sem.at[k], recv_sem=recv_sem.at[me],
            device_id={"dp": to}, device_id_type=pl.DeviceIdType.MESH)

    def arrival(k):
        source = lax.rem(me + n - k, n)
        return pltpu.make_async_remote_copy(
            src_ref=msg.at[me], dst_ref=recv.at[source], send_sem=send_sem.at[k], recv_sem=recv_sem.at[source],
            device_id={"dp": source}, device_id_type=pl.DeviceIdType.MESH)

    for k in range(1, n):
        send(k).start()
    own_copy = pltpu.make_async_copy(msg.at[me], recv.at[me], own_sem)
    own_copy.start()
    for q in range(flat_rows):
        pgv[:, q * LANES:(q + 1) * LANES] = flatv[:, q, :].astype(jnp.bfloat16)
    pg_copy = pltpu.make_async_copy(pgv, pg_ref, pg_sem)
    pg_copy.start()
    for k in range(1, n):
        arrival(k).wait_recv()

    for k in range(1, n):
        send(k).wait_send()
    own_copy.wait()
    pg_copy.wait()


def gram(n, ex, own_rows, flat_width, recv, pg_in, fisher_ref, pg_ref, outv, out_sem, pg_sem):
    left = FCOLS // LANES
    seg = max(1, own_rows // LANES)
    stat = ex * (left + seg)
    pg_copy = pltpu.make_async_copy(pg_in, pg_ref, pg_sem)
    pg_copy.start()

    def rows(first, step):
        return jnp.concatenate([recv[:, first + e * step, :] for e in range(ex)], axis=0)

    total = jnp.sum(recv[:, stat, :], keepdims=True)
    scale = flat_width / (total + EPSILON)
    lhs = jnp.concatenate([rows(ex * left + q, seg) for q in range(seg)], axis=1) * scale
    lhs_high, lhs_low = split(lhs)
    lhs = jnp.concatenate([lhs_high, lhs_high, lhs_low], axis=0)
    rhs_high, rhs_low = split(jnp.concatenate([rows(j, left) for j in range(left)], axis=1))
    rhs = jnp.concatenate([rhs_high, rhs_low, rhs_high], axis=0)
    copies = []
    if own_rows % LANES:
        outv[...] = lax.dot_general(lhs, rhs, TN, preferred_element_type=jnp.float32)
        me = lax.axis_index("dp")
        first = pl.multiple_of(lax.rem(me * own_rows, LANES), own_rows)
        copies.append(pltpu.make_async_copy(outv.at[pl.ds(first, own_rows)], fisher_ref, out_sem.at[0]))
        copies[-1].start()
    else:
        for i in range(seg):
            span = slice(i * LANES, (i + 1) * LANES)
            outv[span] = lax.dot_general(lhs[:, span], rhs, TN, preferred_element_type=jnp.float32)
            copies.append(pltpu.make_async_copy(outv.at[span], fisher_ref.at[span], out_sem.at[i]))
            copies[-1].start()
    pg_copy.wait()
    for copy in copies:
        copy.wait()


def local(n, stored_inputs, output_grads, basis_in, basis_out, ex_weight):
    ex, seq, ff = stored_inputs.shape
    width = output_grads.shape[2]
    rank_in, rank_out = basis_in.shape[1], basis_out.shape[1]
    flat_width = rank_in * rank_out
    own_rows = flat_width // n
    seg = max(1, own_rows // LANES)
    x_cuts, g_cuts = cut(ff, 2048), cut(width, 2048)
    msg_rows = -(-(ex * (FCOLS // LANES + seg) + 1) // 8) * 8
    any_spec = pl.BlockSpec(memory_space=pl.ANY)
    bf16, f32 = jnp.bfloat16, jnp.float32
    dma = pltpu.SemaphoreType.DMA
    vmem_spec = pl.BlockSpec(memory_space=pltpu.VMEM)
    flat_grads = jax.ShapeDtypeStruct((ex, flat_width), bf16)
    operands = (stored_inputs.reshape(ex * seq, ff), output_grads.reshape(ex * seq, width), basis_in.T, basis_out.T, ex_weight)
    recv, grads = pl.pallas_call(
        functools.partial(exchange, n, ex, own_rows, x_cuts, g_cuts),
        out_shape=(jax.ShapeDtypeStruct((n, msg_rows, LANES), f32), flat_grads),
        in_specs=[any_spec] * 5,
        out_specs=(any_spec, any_spec),
        scratch_shapes=[
            pltpu.VMEM((ex * seq, ff), bf16),
            pltpu.VMEM((ex * seq, width), bf16),
            pltpu.VMEM((rank_in, ff), bf16),
            pltpu.VMEM((rank_out, width), bf16),
            pltpu.SMEM((ex,), f32),
            pltpu.VMEM((ex, rank_out, rank_in), f32),
            pltpu.VMEM((ex, flat_width // LANES, LANES), f32),
            pltpu.VMEM((n, msg_rows, LANES), f32),
            pltpu.VMEM((ex, flat_width), bf16),
            dma((len(x_cuts),)), dma((len(x_cuts),)), dma((len(g_cuts),)), dma((len(g_cuts),)),
            dma((n,)), dma((n,)), dma(()), dma(()), dma(()),
        ],
        compiler_params=pltpu.CompilerParams(
            collective_id=0, has_side_effects=True, vmem_limit_bytes=40 * 1024 * 1024),
    )(*(pltpu.with_memory_space_constraint(operand, pltpu.HBM) for operand in operands))
    return pl.pallas_call(
        functools.partial(gram, n, ex, own_rows, flat_width),
        out_shape=(jax.ShapeDtypeStruct((own_rows, FCOLS), f32), flat_grads),
        in_specs=[vmem_spec, any_spec],
        out_specs=(any_spec, any_spec),
        scratch_shapes=[pltpu.VMEM((seg * LANES, FCOLS), f32), dma((seg,)), dma(())],
        compiler_params=pltpu.CompilerParams(vmem_limit_bytes=16 * 1024 * 1024),
    )(recv, grads)


def solution(mesh):
    in_specs = (
        P(("groups", "dp"), None, None),
        P(("groups", "dp"), None, None),
        P(),
        P(),
        P(("groups", "dp")),
    )
    out_specs = (P(("groups", "dp"), None), P(("groups", "dp"), None))
    return jax.shard_map(functools.partial(local, mesh.shape["dp"]), mesh=mesh, in_specs=in_specs, out_specs=out_specs, check_vma=False)
```

```python
import functools

import jax
import jax.numpy as jnp
from jax import lax
from jax.experimental import pallas as pl
from jax.experimental.pallas import tpu as pltpu
from jax.sharding import PartitionSpec as P

FCOLS = 1024
LANES = 128
CHUNK = 2048
WINDOW = 4
EPSILON = 1e-6
NT = (((1,), (1,)), ((), ()))
TN = (((0,), (0,)), ((), ()))


def split(value):
    high = value.astype(jnp.bfloat16)
    return high, (value - high.astype(jnp.float32)).astype(jnp.bfloat16)


def exchange(n, ex, own_rows, x_cuts, g_cuts, x_ref, g_ref, bi_ref, bo_ref, w_ref, recv, pg_ref,
           xv, gv, biv, bov, wv, pv, blk, flatv, msg, pgv,
           xs, bis, gs, bos, send_sem, recv_sem, own_sem, pg_sem, w_sem):
    me = lax.axis_index("dp")
    tokens = x_ref.shape[0] // ex
    rank_in, rank_out = bi_ref.shape[0], bo_ref.shape[0]
    left = FCOLS // LANES
    flat_rows = rank_in * rank_out // LANES
    seg = max(1, own_rows // LANES)
    stat = ex * (left + seg)

    x_set, g_set = ((x_ref, xv, xs), (bi_ref, biv, bis)), ((g_ref, gv, gs), (bo_ref, bov, bos))

    def span_of(at):
        return pl.ds(pl.multiple_of(at * CHUNK, CHUNK), CHUNK)

    def load(ref, buf, sem, at):
        return pltpu.make_async_copy(ref.at[:, span_of(at)], buf.at[:, span_of(at)], sem.at[at])

    def issue(at):
        for pair, first, last in ((x_set, 0, x_cuts), (g_set, x_cuts, x_cuts + g_cuts)):
            @pl.when((at >= first) & (at < last))
            def _():
                load(*pair[1], at - first).start()
                load(*pair[0], at - first).start()

    def each(first, last, body):
        def step(at, carry):
            body(at)
            return carry
        lax.fori_loop(first, last, step, 0)

    each(0, WINDOW, issue)
    w_copy = pltpu.make_async_copy(w_ref, wv, w_sem)
    w_copy.start()

    barrier = pltpu.get_barrier_semaphore()

    @functools.partial(each, 1, n)
    def _(k):
        pl.semaphore_signal(barrier, inc=1, device_id={"dp": lax.rem(me + k, n)}, device_id_type=pl.DeviceIdType.MESH)

    def project(pair, first, count, slot):
        (_, data, _), (_, basis, _) = pair

        def step(at, total):
            load(*pair[1], at).wait()
            load(*pair[0], at).wait()
            issue(first + at + WINDOW)
            return total + lax.dot_general(
                basis[:, span_of(at)], data[:, span_of(at)], NT, preferred_element_type=jnp.float32)

        total = lax.fori_loop(0, count, step, jnp.zeros((basis.shape[0], data.shape[0]), jnp.float32))
        pv[slot, :basis.shape[0]] = total.astype(jnp.bfloat16)

    project(x_set, 0, x_cuts, 0)
    project(g_set, x_cuts, g_cuts, 1)

    w_copy.wait()
    pl.semaphore_wait(barrier, n - 1)
    trace = None
    for e in range(ex):
        span = slice(e * tokens, (e + 1) * tokens)
        blk[e] = lax.dot_general(pv[1, :rank_out, span], pv[0, :rank_in, span], NT, preferred_element_type=jnp.float32)
    for e in range(ex):
        per = LANES // rank_in
        flat = jnp.concatenate([blk[e, pl.ds(p, flat_rows, per), :] for p in range(per)], axis=1)
        weighted = flat * wv[e]
        flatv[e] = flat
        term = jnp.sum(weighted * flat, axis=0, keepdims=True)
        trace = term if trace is None else trace + term
        for d in range(n):
            first = d * own_rows // LANES
            msg[d, e * left:(e + 1) * left] = flat[:left]
            msg[d, ex * left + e * seg:ex * left + (e + 1) * seg] = weighted[first:first + seg]
    for d in range(n):
        msg[d, stat:stat + 1] = trace


    def send(k):
        to = lax.rem(me + k, n)
        return pltpu.make_async_remote_copy(
            src_ref=msg.at[to], dst_ref=recv.at[me], send_sem=send_sem.at[k], recv_sem=recv_sem.at[me],
            device_id={"dp": to}, device_id_type=pl.DeviceIdType.MESH)

    def arrival(k):
        source = lax.rem(me + n - k, n)
        return pltpu.make_async_remote_copy(
            src_ref=msg.at[me], dst_ref=recv.at[source], send_sem=send_sem.at[k], recv_sem=recv_sem.at[source],
            device_id={"dp": source}, device_id_type=pl.DeviceIdType.MESH)

    each(1, n, lambda k: send(k).start())
    own_copy = pltpu.make_async_copy(msg.at[me], recv.at[me], own_sem)
    own_copy.start()
    for q in range(flat_rows):
        pgv[:, q * LANES:(q + 1) * LANES] = flatv[:, q, :].astype(jnp.bfloat16)
    pg_copy = pltpu.make_async_copy(pgv, pg_ref, pg_sem)
    pg_copy.start()
    each(1, n, lambda k: arrival(k).wait_recv())

    each(1, n, lambda k: send(k).wait_send())
    own_copy.wait()
    pg_copy.wait()


def gram(n, ex, own_rows, flat_width, recv, pg_in, fisher_ref, pg_ref, outv, out_sem, pg_sem):
    left = FCOLS // LANES
    seg = max(1, own_rows // LANES)
    stat = ex * (left + seg)
    pg_copy = pltpu.make_async_copy(pg_in, pg_ref, pg_sem)
    pg_copy.start()

    def rows(first, step):
        return jnp.concatenate([recv[:, first + e * step, :] for e in range(ex)], axis=0)

    total = jnp.sum(recv[:, stat, :], keepdims=True)
    scale = flat_width / (total + EPSILON)
    lhs = jnp.concatenate([rows(ex * left + q, seg) for q in range(seg)], axis=1) * scale
    lhs_high, lhs_low = split(lhs)
    lhs = jnp.concatenate([lhs_high, lhs_high, lhs_low], axis=0)
    rhs_high, rhs_low = split(jnp.concatenate([rows(j, left) for j in range(left)], axis=1))
    rhs = jnp.concatenate([rhs_high, rhs_low, rhs_high], axis=0)
    copies = []
    if own_rows % LANES:
        outv[...] = lax.dot_general(lhs, rhs, TN, preferred_element_type=jnp.float32)
        me = lax.axis_index("dp")
        first = pl.multiple_of(lax.rem(me * own_rows, LANES), own_rows)
        copies.append(pltpu.make_async_copy(outv.at[pl.ds(first, own_rows)], fisher_ref, out_sem.at[0]))
        copies[-1].start()
    else:
        for i in range(seg):
            span = slice(i * LANES, (i + 1) * LANES)
            outv[span] = lax.dot_general(lhs[:, span], rhs, TN, preferred_element_type=jnp.float32)
            copies.append(pltpu.make_async_copy(outv.at[span], fisher_ref.at[span], out_sem.at[i]))
            copies[-1].start()
    pg_copy.wait()
    for copy in copies:
        copy.wait()


def local(n, stored_inputs, output_grads, basis_in, basis_out, ex_weight):
    ex, seq, ff = stored_inputs.shape
    width = output_grads.shape[2]
    rank_in, rank_out = basis_in.shape[1], basis_out.shape[1]
    flat_width = rank_in * rank_out
    own_rows = flat_width // n
    seg = max(1, own_rows // LANES)
    x_cuts, g_cuts = ff // CHUNK, width // CHUNK
    msg_rows = -(-(ex * (FCOLS // LANES + seg) + 1) // 8) * 8
    any_spec = pl.BlockSpec(memory_space=pl.ANY)
    bf16, f32 = jnp.bfloat16, jnp.float32
    dma = pltpu.SemaphoreType.DMA
    vmem_spec = pl.BlockSpec(memory_space=pltpu.VMEM)
    flat_grads = jax.ShapeDtypeStruct((ex, flat_width), bf16)
    operands = (stored_inputs.reshape(ex * seq, ff), output_grads.reshape(ex * seq, width), basis_in.T, basis_out.T, ex_weight)
    recv, grads = pl.pallas_call(
        functools.partial(exchange, n, ex, own_rows, x_cuts, g_cuts),
        out_shape=(jax.ShapeDtypeStruct((n, msg_rows, LANES), f32), flat_grads),
        in_specs=[any_spec] * 5,
        out_specs=(any_spec, any_spec),
        scratch_shapes=[
            pltpu.VMEM((ex * seq, ff), bf16),
            pltpu.VMEM((ex * seq, width), bf16),
            pltpu.VMEM((rank_in, ff), bf16),
            pltpu.VMEM((rank_out, width), bf16),
            pltpu.SMEM((ex,), f32),
            pltpu.VMEM((2, max(rank_in, rank_out), ex * seq), bf16),
            pltpu.VMEM((ex, rank_out, rank_in), f32),
            pltpu.VMEM((ex, flat_width // LANES, LANES), f32),
            pltpu.VMEM((n, msg_rows, LANES), f32),
            pltpu.VMEM((ex, flat_width), bf16),
            dma((x_cuts,)), dma((x_cuts,)), dma((g_cuts,)), dma((g_cuts,)),
            dma((n,)), dma((n,)), dma(()), dma(()), dma(()),
        ],
        compiler_params=pltpu.CompilerParams(
            collective_id=0, has_side_effects=True, vmem_limit_bytes=40 * 1024 * 1024),
    )(*(pltpu.with_memory_space_constraint(operand, pltpu.HBM) for operand in operands))
    return pl.pallas_call(
        functools.partial(gram, n, ex, own_rows, flat_width),
        out_shape=(jax.ShapeDtypeStruct((own_rows, FCOLS), f32), flat_grads),
        in_specs=[vmem_spec, any_spec],
        out_specs=(any_spec, any_spec),
        scratch_shapes=[pltpu.VMEM((seg * LANES, FCOLS), f32), dma((seg,)), dma(())],
        compiler_params=pltpu.CompilerParams(vmem_limit_bytes=16 * 1024 * 1024),
    )(recv, grads)


def solution(mesh):
    in_specs = (
        P(("groups", "dp"), None, None),
        P(("groups", "dp"), None, None),
        P(),
        P(),
        P(("groups", "dp")),
    )
    out_specs = (P(("groups", "dp"), None), P(("groups", "dp"), None))
    return jax.shard_map(functools.partial(local, mesh.shape["dp"]), mesh=mesh, in_specs=in_specs, out_specs=out_specs, check_vma=False)
```
